32 devices in a mesh: seq: 8 (over z, y), head: 4 (over x, core).
Axes of the slice: x: 2, y: 2, z: 4, core: 2. Of those that a mesh axis runs over, the one named last changes fastest.
Arguments:
- hidden_in: bfloat16 [2048, 2048], P('seq'), may hold values from -6 to 6
- attn_gain: float32 [2048], replicated, may hold values from 0.1 to 1.9
- w_qkv: bfloat16 [2048, 3, 2048], P(None, None, 'head'), may hold values from -0.125 to 0.125
- out_gain: float32 [2048], P('head'), may hold values from 0.1 to 1.9
- w_out: bfloat16 [2048, 2048], P('head'), may hold values from -0.125 to 0.125
- moe_gain: float32 [2048], replicated, may hold values from 0.1 to 1.9
- routes: int32 [2048, 8], P(('seq', 'head')), may hold values from 0 to 63, all different within a row; in each aligned block of 64 rows (0 to 63, 64 to 127, ...) at most 9 rows name the same one
- gate_weights: float32 [2048, 8], P(('seq', 'head')), may hold values from 0.1 to 0.6
- w_gate_up: bfloat16 [64, 2, 2048, 1024], P('seq', None, None, 'head'), may hold values from -0.125 to 0.125
- w_down: bfloat16 [64, 1024, 2048], P('seq', 'head'), may hold values from -0.1875 to 0.1875
Outputs:
- layer_out: bfloat16 [2048, 2048], P(('seq', 'head'))
The draws below stay inside these ranges and needn't reach their ends.
Inputs may be any that keep to these rules, and one draw needn't show every extreme that they name: `routes`: each row names 8 different experts; within each aligned block of 64 rows (the rows of one device) no expert is named more than 9 times, a bound that some block reaches.
All inputs are finite; a program needn't handle non-finite values.
Results may differ from the reference program's by a relative error of at most 0.015.
Values may be sent and summed in bfloat16 or wider, within the bound.
A program may use at most 128 MiB of HBM per device.

```python
import math
import jax
import jax.numpy as jnp
import numpy as np
from jax import lax

D = 2048
H = 16
DH = 128
FF = 1024
EXPERTS = 64
TOP = 8
TOK_DEV = 256
HD = 2048
ROWS = 64
CAP = 9
TOKENS = 2048
N_HEAD = 4


def level_of(key, shape, split, least, top_value):
    level = 1.0
    for dim, shards_of in split:
        draws = jax.random.uniform(jax.random.fold_in(jax.random.fold_in(key, 6), dim), (shards_of,), jnp.float32, least / len(split), top_value / len(split))
        level = level * jnp.repeat(jnp.exp(draws), shape[dim] // shards_of).reshape((-1,) + (1,) * (len(shape) - 1 - dim))
    return level


def assign_block(key, own, number, rows, number_of, top, limit, skew):
    order = jax.random.permutation(key, number_of)
    packed, common = shares(number_of, rows * top, limit, skew, True), shares(number_of, rows * top, limit, skew, False)
    places = jnp.arange(number_of)

    def named(lengths, offset_by):
        used = int((lengths > 0).sum())
        fixed = max(1, used // 4)
        shifted = fixed + (places - fixed + offset_by * (used - fixed)) % max(1, number_of - fixed)
        return jnp.zeros((number_of,), jnp.int32).at[order[jnp.where(places < fixed, places, shifted)]].set(jnp.asarray(lengths, jnp.int32))

    lengths = jnp.where(number % 4 == 0, named(packed, number // 4), named(common, number - number // 4 - 1))
    mixed = jax.random.permutation(jax.random.fold_in(own, 3), number_of)
    source_of, sink = mixed[0:number_of // 2 * 2:2], mixed[1:number_of // 2 * 2:2]
    margin = jnp.minimum(lengths[source_of] - 1, limit - lengths[sink]) // 2
    margin = jnp.where((source_of == order[0]) | (sink == order[0]) | (lengths[sink] == 0), 0, jnp.maximum(margin, 0))
    shifted = jax.random.randint(jax.random.fold_in(own, 4), (number_of // 2,), 0, 1 << 20) % (margin + 1)
    lengths = lengths.at[source_of].add(-shifted).at[sink].add(shifted)
    labels = jnp.searchsorted(jnp.cumsum(lengths), jnp.arange(rows * top), side="right").astype(jnp.int32)
    table = labels.reshape(top, rows).T
    table = table[jax.random.permutation(jax.random.fold_in(own, 1), rows)]
    offset_by = jax.random.randint(jax.random.fold_in(own, 2), (rows, 1), 0, top)
    return jnp.take_along_axis(table, (jnp.arange(top)[None, :] + offset_by) % top, axis=1)


def shares(number_of, total, reach, lean, full):
    loads = [(1 << 20) // math.isqrt(standing ** lean) + 1 for standing in range(1, number_of + 1)]
    largest = reach if full else min(reach, max(-(-total // number_of), total * loads[0] // sum(loads)))
    least = 1 if total - largest >= number_of - 1 else 0
    holding, spare = [largest] + [least] * (number_of - 1), total - largest - least * (number_of - 1)
    while spare > 0:
        movable = [i for i in range(1, number_of) if holding[i] < largest] or [i for i in range(1, number_of) if holding[i] < reach]
        whole, left = sum([loads[i] for i in movable]), spare
        for i in movable:
            addition = min(reach - holding[i], max(1, left * loads[i] // whole), spare)
            holding[i] = holding[i] + addition
            spare = spare - addition
    return np.array(holding)


def gaussian(stream_key, dims, width, bound, pieces=(), kind=jnp.bfloat16):
    drawn = width * jax.random.normal(stream_key, dims, jnp.float32)
    if pieces:
        drawn = drawn * level_of(stream_key, dims, pieces, -0.22, 0.18)
    return jnp.clip(drawn, -bound, bound).astype(kind)


def setup_inputs(seed: int = 0) -> dict:
    keys = jax.random.split(jax.random.key(seed), 11)
    hidden_in = gaussian(keys[0], (TOKENS, D), 1.0, 6.0, ((0, 8),))
    attn_gain = jnp.clip(1.0 + 0.18 * jax.random.normal(keys[1], (D,), jnp.float32), 0.1, 1.9)
    w_qkv = gaussian(keys[2], (D, 3, HD), D ** -0.5, 0.125, ((2, 4),))
    out_gain = jnp.clip(1.0 + 0.18 * jax.random.normal(keys[3], (HD,), jnp.float32), 0.1, 1.9)
    w_out = gaussian(keys[4], (HD, D), HD ** -0.5, 0.125, ((0, 4),))
    moe_gain = jnp.clip(1.0 + 0.18 * jax.random.normal(keys[5], (D,), jnp.float32), 0.1, 1.9)
    routes_keys = jax.random.split(jax.random.fold_in(keys[6], 1), TOKENS // ROWS)
    routes_turns = jax.random.permutation(jax.random.fold_in(keys[6], 3), TOKENS // ROWS)
    routes = jax.vmap(lambda own, number: assign_block(jax.random.fold_in(keys[6], 2), own, number, ROWS, EXPERTS, TOP, CAP, 2))(routes_keys, routes_turns).reshape((TOKENS, TOP))
    gate_weights = jnp.clip(jnp.exp(math.log(0.6) - 1.7917595 * jax.random.uniform(keys[7], (TOKENS, TOP), jnp.float32) ** level_of(keys[7], (TOKENS, TOP), ((0, 32),), -0.2, 0.2)), 0.1, 0.6)
    w_gate_up = gaussian(keys[8], (EXPERTS, 2, D, FF), D ** -0.5, 0.125, ((0, 8), (3, 4)))
    w_down = gaussian(keys[9], (EXPERTS, FF, D), FF ** -0.5, 0.1875, ((0, 8), (1, 4)))
    return {"hidden_in": hidden_in, "attn_gain": attn_gain, "w_qkv": w_qkv, "out_gain": out_gain, "w_out": w_out, "moe_gain": moe_gain, "routes": routes, "gate_weights": gate_weights, "w_gate_up": w_gate_up, "w_down": w_down}


EPSILON = 1e-06

def rms_norm(values, gain):
    mean_square = lax.optimization_barrier(jnp.mean(values * values, axis=-1, keepdims=True))
    return values * lax.rsqrt(mean_square + EPSILON) * gain

def slot_table(route_rows):
    flat_routes = route_rows.reshape(-1)
    experts_iota = jnp.arange(EXPERTS, dtype=jnp.int32)
    onehot = (flat_routes[:, None] == experts_iota[None, :]).astype(jnp.int32)
    before = jnp.cumsum(onehot, axis=0) - onehot
    position = lax.optimization_barrier(jnp.sum(before * onehot, axis=1))
    return position.reshape(route_rows.shape)

def reference(hidden_in, attn_gain, w_qkv, out_gain, w_out, moe_gain, routes, gate_weights, w_gate_up, w_down):
    highest = lax.Precision.HIGHEST
    resid_in = hidden_in.astype(jnp.float32)
    normed = rms_norm(resid_in, attn_gain).astype(jnp.bfloat16)
    projected = jnp.dot(normed, w_qkv.reshape(D, 3 * HD), preferred_element_type=jnp.float32)
    projected = projected.astype(jnp.bfloat16).reshape(TOKENS, 3, H, DH)
    block_total = TOKENS // TOK_DEV
    query = projected[:, 0].reshape(block_total, TOK_DEV, H, DH)
    keys_all = projected[:, 1].reshape(block_total, TOK_DEV, H, DH)
    values_all = projected[:, 2].reshape(block_total, TOK_DEV, H, DH)
    causal = jnp.tril(jnp.ones((TOK_DEV, TOK_DEV), jnp.float32))

    def block_step(carried, inputs):
        query_blk, key_blk, value_blk = inputs
        query32 = query_blk.astype(jnp.float32)
        key32 = key_blk.astype(jnp.float32)
        value32 = value_blk.astype(jnp.float32)
        scores = jnp.einsum('thd,shd->hts', query32, key32, precision=highest) * causal
        scores = scores.astype(jnp.bfloat16).astype(jnp.float32)
        local_part = jnp.einsum('hts,shd->thd', scores, value32, precision=highest)
        remote_part = jnp.einsum('thd,hde->the', query32, carried, precision=highest)
        new_state = carried + jnp.einsum('thd,the->hde', key32, value32, precision=highest)
        return (new_state, local_part + remote_part)
    start_state = jnp.zeros((H, DH, DH), jnp.float32)
    final_state, attended = lax.scan(block_step, start_state, (query, keys_all, values_all))
    attended = attended.reshape(TOKENS, H, DH)
    head_square = lax.optimization_barrier(jnp.mean(attended * attended, axis=-1, keepdims=True))
    mixed = (attended * lax.rsqrt(head_square + EPSILON)).reshape(TOKENS, HD) * out_gain
    mixed = mixed.astype(jnp.bfloat16)
    resid = resid_in + jnp.dot(mixed, w_out, preferred_element_type=jnp.float32)
    normed2 = rms_norm(resid, moe_gain).astype(jnp.bfloat16)
    group_count = TOKENS // ROWS
    position = jax.vmap(slot_table)(routes.reshape(group_count, ROWS, TOP)).reshape(TOKENS, TOP)
    group_ids = (jnp.arange(TOKENS, dtype=jnp.int32) // ROWS)[:, None]
    flat_index = (routes * (group_count * CAP) + group_ids * CAP + position).astype(jnp.int32)
    token_ids = jnp.repeat(jnp.arange(TOKENS, dtype=jnp.int32), TOP)
    table = jnp.full((EXPERTS * group_count * CAP,), TOKENS, jnp.int32)
    table = table.at[flat_index.reshape(-1)].set(token_ids)
    padded = jnp.concatenate([normed2, jnp.zeros((1, D), jnp.bfloat16)], axis=0)
    quarter = FF // N_HEAD

    def run_expert(inputs):
        table_rows, gate_up, down_rows = inputs
        rows_in = padded[table_rows]
        gate_val = jnp.dot(rows_in, gate_up[0], preferred_element_type=jnp.float32)
        up_val = jnp.dot(rows_in, gate_up[1], preferred_element_type=jnp.float32)
        hidden_units = (jax.nn.silu(gate_val) * up_val).astype(jnp.bfloat16)
        total = jnp.zeros((rows_in.shape[0], D), jnp.float32)
        for group_idx in range(N_HEAD):
            part = jnp.dot(hidden_units[:, group_idx * quarter:(group_idx + 1) * quarter], down_rows[group_idx * quarter:(group_idx + 1) * quarter], preferred_element_type=jnp.float32)
            total = total + part.astype(jnp.bfloat16).astype(jnp.float32)
        return total.astype(jnp.bfloat16)
    expert_rows = lax.map(run_expert, (table.reshape(EXPERTS, group_count * CAP), w_gate_up, w_down))
    picked = expert_rows.reshape(EXPERTS * group_count * CAP, D)[flat_index]
    moe_sum = lax.optimization_barrier(jnp.sum(gate_weights[:, :, None] * picked.astype(jnp.float32), axis=1))
    return (resid + moe_sum).astype(jnp.bfloat16)
```

```python
import jax
import jax.numpy as jnp
from jax import lax
from jax.sharding import PartitionSpec as P

D = 2048
DH = 128
EXPERTS = 64
TOP = 8


EPSILON = 1e-06


def rms_norm(values, gain):
    mean_square = jnp.mean(values * values, axis=-1, keepdims=True)
    return values * lax.rsqrt(mean_square + EPSILON) * gain


def expert_tables(routes, gate_weights, exp_local, group_size, capacity):
    both = jnp.concatenate([routes.astype(jnp.float32), gate_weights], axis=1)
    both = lax.all_gather(both, ("seq", "head"), axis=0, tiled=True)
    groups = both.shape[0] // group_size
    expert_ids = lax.axis_index("seq") * exp_local + jnp.arange(exp_local, dtype=jnp.int32)
    match = both[:, None, :TOP] == expert_ids.astype(jnp.float32)[None, :, None]
    member = jnp.any(match, axis=2).reshape(groups, group_size, exp_local)
    weight = jnp.sum(jnp.where(match, both[:, None, TOP:], 0.0), axis=2)
    weight = weight.reshape(groups, group_size, exp_local)
    lower = jnp.tril(jnp.ones((group_size, group_size), jnp.bfloat16), -1)
    before = jnp.einsum(
        "ts,gsj->gjt", lower, member.astype(jnp.bfloat16), preferred_element_type=jnp.float32
    )
    member_t = jnp.transpose(member, (0, 2, 1))
    weight_t = jnp.transpose(weight, (0, 2, 1))
    places = jnp.arange(capacity, dtype=jnp.float32)
    picks = (before[:, :, None, :] == places[:, None]) & member_t[:, :, None, :]
    row_weight = jnp.sum(jnp.where(picks, weight_t[:, :, None, :], 0.0), axis=3)
    return picks.astype(jnp.bfloat16), row_weight


def on_device(
    hidden_in, attn_gain, w_qkv, out_gain, w_out, moe_gain, routes, gate_weights, w_gate_up, w_down
):
    token_count = hidden_in.shape[0]
    head_count = w_qkv.shape[2] // DH
    seq_size = lax.axis_size("seq")
    head_size = lax.axis_size("head")
    exp_local = w_gate_up.shape[0]
    row_count = token_count // head_size
    capacity = max(2, 9 * row_count * TOP // (8 * EXPERTS))
    blocks = 8
    group_size = blocks * row_count
    picks, row_weight = expert_tables(
        routes, gate_weights, exp_local, group_size, blocks * capacity
    )
    resid_in = hidden_in.astype(jnp.float32)
    normed = rms_norm(resid_in, attn_gain).astype(jnp.bfloat16)
    query, keys_local, values_local = (
        jnp.dot(normed, w_qkv[:, c], preferred_element_type=jnp.float32)
        .astype(jnp.bfloat16)
        .reshape(token_count, head_count, DH)
        for c in range(3)
    )
    causal = jnp.tril(jnp.ones((token_count, token_count), jnp.float32))
    scores = (
        jnp.einsum("thd,shd->hts", query, keys_local, preferred_element_type=jnp.float32) * causal
    )
    local_part = jnp.einsum(
        "hts,shd->thd",
        scores.astype(jnp.bfloat16),
        values_local,
        preferred_element_type=jnp.float32,
    )
    own_state = jnp.einsum(
        "thd,the->hde", keys_local, values_local, preferred_element_type=jnp.float32
    )
    seq_index = lax.axis_index("seq")
    piece = lax.all_gather(own_state.astype(jnp.bfloat16), "seq", axis=0, tiled=True).astype(
        jnp.float32
    )
    shard_count = piece.shape[0] // head_count
    stacked = piece.reshape(shard_count, head_count, DH, DH)
    shard_ids = jnp.arange(shard_count, dtype=jnp.int32)
    keep = (shard_ids < seq_index)[:, None, None, None]
    earlier = jnp.zeros_like(own_state) + jnp.sum(jnp.where(keep, stacked, 0.0), axis=0)
    remote_part = jnp.einsum(
        "thd,hde->the", query.astype(jnp.float32), earlier, precision=lax.Precision.HIGHEST
    )
    attended = local_part + remote_part
    head_square = jnp.mean(attended * attended, axis=-1, keepdims=True)
    mixed = (attended * lax.rsqrt(head_square + EPSILON)).reshape(
        token_count, head_count * DH
    ) * out_gain
    mixed = mixed.astype(jnp.bfloat16)
    attn_rows = lax.psum_scatter(
        jnp.dot(mixed, w_out, preferred_element_type=jnp.float32).astype(jnp.bfloat16),
        "head",
        scatter_dimension=0,
        tiled=True,
    ).astype(jnp.float32)
    resid = (
        lax.dynamic_slice_in_dim(resid_in, lax.axis_index("head") * row_count, row_count, 0)
        + attn_rows
    )
    normed2 = rms_norm(resid, moe_gain).astype(jnp.bfloat16)
    everyone = lax.all_gather(normed2, ("seq", "head"), axis=0, tiled=True)
    everyone = everyone.reshape(-1, group_size, D)
    rows_in = jnp.einsum(
        "gjct,gtd->jgcd", picks, everyone, preferred_element_type=jnp.float32
    ).astype(jnp.bfloat16)
    gate_val = jnp.einsum(
        "jgcd,jdf->jgcf", rows_in, w_gate_up[:, 0], preferred_element_type=jnp.float32
    )
    up_val = jnp.einsum(
        "jgcd,jdf->jgcf", rows_in, w_gate_up[:, 1], preferred_element_type=jnp.float32
    )
    weights = jnp.transpose(row_weight, (1, 0, 2))[..., None]
    hidden_units = (jax.nn.silu(gate_val) * up_val * weights).astype(jnp.bfloat16)
    rows_out = jnp.einsum(
        "jgcf,jfd->jgcd", hidden_units, w_down, preferred_element_type=jnp.float32
    ).astype(jnp.bfloat16)
    partial = jnp.einsum(
        "gjct,jgcd->gtd", picks, rows_out, preferred_element_type=jnp.float32
    ).astype(jnp.bfloat16)
    moe_sum = lax.psum_scatter(
        partial.reshape(-1, D), ("seq", "head"), scatter_dimension=0, tiled=True
    )
    return (resid + moe_sum.astype(jnp.float32)).astype(jnp.bfloat16)


def solution(mesh):
    placed = (
        P("seq", None),
        P(),
        P(None, None, "head"),
        P("head"),
        P("head", None),
        P(),
        P(("seq", "head"), None),
        P(("seq", "head"), None),
        P("seq", None, None, "head"),
        P("seq", "head", None),
    )
    return jax.shard_map(
        on_device, mesh=mesh, in_specs=placed, out_specs=P(("seq", "head"), None), check_vma=False
    )
```

```python
import functools
import jax
import jax.numpy as jnp
from jax import lax
from jax.experimental import pallas as pl
from jax.experimental.pallas import tpu as pltpu
from jax.sharding import PartitionSpec as P

D = 2048
DH = 128
EXPERTS = 64
TOP = 8


EPSILON = 1e-06


def rms_norm(values, gain):
    mean_square = jnp.mean(values * values, axis=-1, keepdims=True)
    return values * lax.rsqrt(mean_square + EPSILON) * gain


def axis_bits(name):
    return [(name, bit) for bit in reversed(range(lax.axis_size(name).bit_length() - 1))]


def own_bit(axis_and_bit):
    name, bit = axis_and_bit
    return (lax.axis_index(name) // (1 << bit)) % 2


def partner(axis_and_bit):
    name, bit = axis_and_bit
    return {name: lax.axis_index(name) + (1 - 2 * own_bit(axis_and_bit)) * (1 << bit)}


def greet(bits):
    barrier = pltpu.get_barrier_semaphore()
    for item in bits:
        pl.semaphore_signal(
            barrier, inc=1, device_id=partner(item), device_id_type=pl.DeviceIdType.MESH
        )
    pl.semaphore_wait(barrier, len(bits))


def halving_orders(bits):
    count = len(bits)
    first = list(reversed(range(count)))
    heads = [d for d in first if bits[d][0] == "head"]
    others = [d for d in first if bits[d][0] != "head"]
    if not heads or not others:
        return [first, first]
    return [first, heads[:1] + others[:1] + heads[1:] + others[1:]]


def gather_kernel(bits, parts, x_ref, out_ref, send_sem, recv_sem, own_sem):
    count = len(bits)
    width = x_ref.shape[1] // parts
    orders = [list(reversed(order)) for order in halving_orders(bits)]
    mine = [own_bit(item) for item in bits]

    def region(done, part):
        index = tuple(slice(None) if d in done else mine[d] for d in range(count))
        return out_ref.at[index + (slice(None), pl.ds(part * width, width))]

    own = pltpu.make_async_copy(x_ref, out_ref.at[tuple(mine)], own_sem)
    own.start()
    greet(bits)
    copies = [[None] * count for _ in range(parts)]
    for stage in range(count):
        for part in range(parts):
            order = orders[part % 2]
            if stage == 1 and part == 0:
                own.wait()
            if stage:
                copies[part][stage - 1].wait_recv()
            place = region(order[:stage], part)
            source = x_ref.at[:, pl.ds(part * width, width)] if stage == 0 else place
            copy = pltpu.make_async_remote_copy(
                src_ref=source,
                dst_ref=place,
                send_sem=send_sem.at[part, stage],
                recv_sem=recv_sem.at[part, stage],
                device_id=partner(bits[order[stage]]),
                device_id_type=pl.DeviceIdType.MESH,
            )
            copy.start()
            copies[part][stage] = copy
    for part in range(parts):
        copies[part][count - 1].wait_recv()
    for part in range(parts):
        for stage in range(count):
            copies[part][stage].wait_send()


def gather(x, bits, parts, collective_id):
    count = len(bits)
    rows, columns = x.shape
    out = pl.pallas_call(
        functools.partial(gather_kernel, bits, parts),
        out_shape=jax.ShapeDtypeStruct((2,) * count + x.shape, x.dtype),
        in_specs=[pl.BlockSpec(memory_space=pl.ANY)],
        out_specs=pl.BlockSpec(memory_space=pl.ANY),
        scratch_shapes=[
            pltpu.SemaphoreType.DMA((parts, count)),
            pltpu.SemaphoreType.DMA((parts, count)),
            pltpu.SemaphoreType.DMA,
        ],
        compiler_params=pltpu.CompilerParams(collective_id=collective_id, has_side_effects=True),
        name=f"gather{collective_id}",
    )(x)
    return out.reshape((1 << count) * rows, columns)


def reduce_kernel(bits, parts, x_ref, out_ref, keep, *rest):
    count = len(bits)
    received, (send_sem, recv_sem, own_sem) = rest[:count], rest[count:]
    width = x_ref.shape[-1] // parts
    orders = halving_orders(bits)
    mine = [own_bit(item) for item in bits]

    def columns(part):
        return (slice(None), pl.ds(part * width, width))

    def kept(done, part, flip=None):
        return tuple(
            (1 - mine[d]) if d == flip else (mine[d] if d in done else slice(None))
            for d in range(count - 1)
        ) + columns(part)

    whole = (slice(None),) * (count - 1)
    own = []
    for part in range(parts):
        copy = pltpu.make_async_copy(
            x_ref.at[whole + (mine[-1],) + columns(part)],
            keep.at[whole + columns(part)],
            own_sem.at[part],
        )
        copy.start()
        own.append(copy)
    greet(bits)
    copies = [[None] * count for _ in range(parts)]
    for stage in range(count + 1):
        for part in range(parts):
            order = orders[part % 2]
            if stage:
                if stage == 1:
                    own[part].wait()
                copies[part][stage - 1].wait_recv()
                place = kept(order[:stage], part)
                piece = (slice(None),) * (count - stage) + columns(part)
                total = keep[place] + received[stage - 1][piece]
                if stage == count:
                    out_ref[:, pl.ds(part * width, width)] = total
                    continue
                keep[place] = total
            if stage == 0:
                source = x_ref.at[whole + (1 - mine[-1],) + columns(part)]
            else:
                source = keep.at[kept(order[:stage], part, order[stage])]
            landing = (slice(None),) * (count - 1 - stage) + columns(part)
            copy = pltpu.make_async_remote_copy(
                src_ref=source,
                dst_ref=received[stage].at[landing],
                send_sem=send_sem.at[part, stage],
                recv_sem=recv_sem.at[part, stage],
                device_id=partner(bits[order[stage]]),
                device_id_type=pl.DeviceIdType.MESH,
            )
            copy.start()
            copies[part][stage] = copy
    for part in range(parts):
        for stage in range(count):
            copies[part][stage].wait_send()


def reduce_scatter(x, bits, parts, collective_id):
    count = len(bits)
    rows, columns = x.shape[0] >> count, x.shape[1]
    block = (rows, columns)
    return pl.pallas_call(
        functools.partial(reduce_kernel, bits, parts),
        out_shape=jax.ShapeDtypeStruct(block, x.dtype),
        in_specs=[pl.BlockSpec(memory_space=pl.ANY)],
        out_specs=pl.BlockSpec(memory_space=pltpu.VMEM),
        scratch_shapes=[pltpu.VMEM((2,) * (count - 1) + block, x.dtype)]
        + [pltpu.VMEM((2,) * (count - 1 - stage) + block, x.dtype) for stage in range(count)]
        + [
            pltpu.SemaphoreType.DMA((parts, count)),
            pltpu.SemaphoreType.DMA((parts, count)),
            pltpu.SemaphoreType.DMA((parts,)),
        ],
        compiler_params=pltpu.CompilerParams(
            collective_id=collective_id,
            has_side_effects=True,
            vmem_limit_bytes=(3 * x.shape[0] * columns + 16 * rows * columns) + (4 << 20),
        ),
        name=f"reduce{collective_id}",
    )(x.reshape((2,) * count + block))


def expert_tables(routes, gate_weights, exp_local, group_size, capacity):
    both = jnp.concatenate([routes.astype(jnp.float32), gate_weights], axis=1)
    rows = both.shape[0]
    both = jnp.pad(both.T, ((0, 0), (0, -rows % 128)))
    both = gather(both, axis_bits("seq") + axis_bits("head"), 1, 0)
    both = jnp.transpose(both.reshape(-1, 2 * TOP, both.shape[1])[:, :, :rows], (0, 2, 1))
    both = both.reshape(-1, 2 * TOP)
    groups = both.shape[0] // group_size
    expert_ids = lax.axis_index("seq") * exp_local + jnp.arange(exp_local, dtype=jnp.int32)
    match = both[:, None, :TOP] == expert_ids.astype(jnp.float32)[None, :, None]
    member = jnp.any(match, axis=2).reshape(groups, group_size, exp_local)
    weight = jnp.sum(jnp.where(match, both[:, None, TOP:], 0.0), axis=2)
    weight = weight.reshape(groups, group_size, exp_local)
    lower = jnp.tril(jnp.ones((group_size, group_size), jnp.bfloat16), -1)
    before = jnp.einsum(
        "ts,gsj->gjt", lower, member.astype(jnp.bfloat16), preferred_element_type=jnp.float32
    )
    member_t = jnp.transpose(member, (0, 2, 1))
    weight_t = jnp.transpose(weight, (0, 2, 1))
    places = jnp.arange(capacity, dtype=jnp.float32)
    picks = (before[:, :, None, :] == places[:, None]) & member_t[:, :, None, :]
    row_weight = jnp.sum(jnp.where(picks, weight_t[:, :, None, :], 0.0), axis=3)
    return picks.astype(jnp.bfloat16), row_weight


def on_device(
    hidden_in, attn_gain, w_qkv, out_gain, w_out, moe_gain, routes, gate_weights, w_gate_up, w_down
):
    token_count = hidden_in.shape[0]
    head_count = w_qkv.shape[2] // DH
    seq_size = lax.axis_size("seq")
    head_size = lax.axis_size("head")
    exp_local = w_gate_up.shape[0]
    row_count = token_count // head_size
    capacity = max(2, 9 * row_count * TOP // (8 * EXPERTS))
    blocks = 8
    group_size = blocks * row_count
    picks, row_weight = expert_tables(
        routes, gate_weights, exp_local, group_size, blocks * capacity
    )
    resid_in = hidden_in.astype(jnp.float32)
    normed = rms_norm(resid_in, attn_gain).astype(jnp.bfloat16)
    query, keys_local, values_local = (
        jnp.dot(normed, w_qkv[:, c], preferred_element_type=jnp.float32)
        .astype(jnp.bfloat16)
        .reshape(token_count, head_count, DH)
        for c in range(3)
    )
    causal = jnp.tril(jnp.ones((token_count, token_count), jnp.float32))
    scores = (
        jnp.einsum("thd,shd->hts", query, keys_local, preferred_element_type=jnp.float32) * causal
    )
    local_part = jnp.einsum(
        "hts,shd->thd",
        scores.astype(jnp.bfloat16),
        values_local,
        preferred_element_type=jnp.float32,
    )
    own_state = jnp.einsum(
        "thd,the->hde", keys_local, values_local, preferred_element_type=jnp.float32
    )
    seq_index = lax.axis_index("seq")
    piece = gather(
        own_state.astype(jnp.bfloat16).reshape(head_count * DH, DH), axis_bits("seq"), 1, 1
    )
    piece = piece.reshape(-1, DH, DH).astype(jnp.float32)
    shard_count = piece.shape[0] // head_count
    stacked = piece.reshape(shard_count, head_count, DH, DH)
    shard_ids = jnp.arange(shard_count, dtype=jnp.int32)
    keep = (shard_ids < seq_index)[:, None, None, None]
    earlier = jnp.zeros_like(own_state) + jnp.sum(jnp.where(keep, stacked, 0.0), axis=0)
    remote_part = jnp.einsum(
        "thd,hde->the", query.astype(jnp.float32), earlier, precision=lax.Precision.HIGHEST
    )
    attended = local_part + remote_part
    head_square = jnp.mean(attended * attended, axis=-1, keepdims=True)
    mixed = (attended * lax.rsqrt(head_square + EPSILON)).reshape(
        token_count, head_count * DH
    ) * out_gain
    mixed = mixed.astype(jnp.bfloat16)
    attn_rows = reduce_scatter(
        jnp.dot(mixed, w_out, preferred_element_type=jnp.float32).astype(jnp.bfloat16),
        axis_bits("head"),
        2,
        2,
    ).astype(jnp.float32)
    resid = (
        lax.dynamic_slice_in_dim(resid_in, lax.axis_index("head") * row_count, row_count, 0)
        + attn_rows
    )
    normed2 = rms_norm(resid, moe_gain).astype(jnp.bfloat16)
    everyone = gather(normed2, axis_bits("seq") + axis_bits("head"), 4, 3)
    everyone = everyone.reshape(-1, group_size, D)
    rows_in = jnp.einsum(
        "gjct,gtd->jgcd", picks, everyone, preferred_element_type=jnp.float32
    ).astype(jnp.bfloat16)
    gate_val = jnp.einsum(
        "jgcd,jdf->jgcf", rows_in, w_gate_up[:, 0], preferred_element_type=jnp.float32
    )
    up_val = jnp.einsum(
        "jgcd,jdf->jgcf", rows_in, w_gate_up[:, 1], preferred_element_type=jnp.float32
    )
    weights = jnp.transpose(row_weight, (1, 0, 2))[..., None]
    hidden_units = (jax.nn.silu(gate_val) * up_val * weights).astype(jnp.bfloat16)
    rows_out = jnp.einsum(
        "jgcf,jfd->jgcd", hidden_units, w_down, preferred_element_type=jnp.float32
    ).astype(jnp.bfloat16)
    partial = jnp.einsum(
        "gjct,jgcd->gtd", picks, rows_out, preferred_element_type=jnp.float32
    ).astype(jnp.bfloat16)
    moe_sum = reduce_scatter(
        partial.reshape(-1, D), axis_bits("seq") + axis_bits("head"), 4, 4
    )
    return (resid + moe_sum.astype(jnp.float32)).astype(jnp.bfloat16)


def solution(mesh):
    placed = (
        P("seq", None),
        P(),
        P(None, None, "head"),
        P("head"),
        P("head", None),
        P(),
        P(("seq", "head"), None),
        P(("seq", "head"), None),
        P("seq", None, None, "head"),
        P("seq", "head", None),
    )
    return jax.shard_map(
        on_device, mesh=mesh, in_specs=placed, out_specs=P(("seq", "head"), None), check_vma=False
    )
```

```python
import functools
import jax
import jax.numpy as jnp
from jax import lax
from jax.experimental import pallas as pl
from jax.experimental.pallas import tpu as pltpu
from jax.sharding import PartitionSpec as P

D = 2048
DH = 128
EXPERTS = 64
TOP = 8


EPSILON = 1e-06


def rms_norm(values, gain):
    mean_square = jnp.mean(values * values, axis=-1, keepdims=True)
    return values * lax.rsqrt(mean_square + EPSILON) * gain


def axis_bits(name):
    return [(name, bit) for bit in reversed(range(lax.axis_size(name).bit_length() - 1))]


def own_bit(axis_and_bit):
    name, bit = axis_and_bit
    return (lax.axis_index(name) // (1 << bit)) % 2


def partner(axis_and_bit):
    name, bit = axis_and_bit
    return {name: lax.axis_index(name) + (1 - 2 * own_bit(axis_and_bit)) * (1 << bit)}


def greet(bits):
    barrier = pltpu.get_barrier_semaphore()
    for item in bits:
        pl.semaphore_signal(
            barrier, inc=1, device_id=partner(item), device_id_type=pl.DeviceIdType.MESH
        )
    pl.semaphore_wait(barrier, len(bits))


def early_kernel(bits, scan_bits, x_ref, state_ref, out_ref, earlier_ref, *scratch):
    everyone, total, sent, landed, send_sem, recv_sem, scan_send, scan_recv, own_sem = scratch
    count = len(bits)
    mine = [own_bit(item) for item in bits]
    own = pltpu.make_async_copy(x_ref, everyone.at[tuple(mine)], own_sem)
    own.start()
    total[...] = state_ref[...]
    earlier_ref[...] = jnp.zeros_like(earlier_ref)
    greet(bits)
    own.wait()
    copies = []
    for stage in range(count):
        dim = count - 1 - stage
        place = everyone.at[tuple(mine[: dim + 1])]
        copy = pltpu.make_async_remote_copy(
            src_ref=place,
            dst_ref=place,
            send_sem=send_sem.at[stage],
            recv_sem=recv_sem.at[stage],
            device_id=partner(bits[dim]),
            device_id_type=pl.DeviceIdType.MESH,
        )
        copy.start()
        copies.append(copy)
        scan = None
        if stage < len(scan_bits):
            item = scan_bits[len(scan_bits) - 1 - stage]
            sent[stage] = total[...].astype(sent.dtype)
            scan = pltpu.make_async_remote_copy(
                src_ref=sent.at[stage],
                dst_ref=landed.at[stage],
                send_sem=scan_send.at[stage],
                recv_sem=scan_recv.at[stage],
                device_id=partner(item),
                device_id_type=pl.DeviceIdType.MESH,
            )
            scan.start()
            copies.append(scan)
        copy.wait_recv()
        if scan is not None:
            scan.wait_recv()
            other = landed[stage].astype(jnp.float32)
            total[...] += other
            earlier_ref[...] += other * own_bit(item).astype(jnp.float32)
    out_ref[...] = everyone[...]
    for copy in copies:
        copy.wait_send()


def early_exchange(x, state, bits, scan_bits, collective_id):
    count, steps = len(bits), len(scan_bits)
    gathered, earlier = pl.pallas_call(
        functools.partial(early_kernel, bits, scan_bits),
        out_shape=[
            jax.ShapeDtypeStruct((2,) * count + x.shape, x.dtype),
            jax.ShapeDtypeStruct(state.shape, jnp.float32),
        ],
        in_specs=[pl.BlockSpec(memory_space=pltpu.VMEM)] * 2,
        out_specs=[pl.BlockSpec(memory_space=pltpu.VMEM)] * 2,
        scratch_shapes=[
            pltpu.VMEM((2,) * count + x.shape, x.dtype),
            pltpu.VMEM(state.shape, jnp.float32),
            pltpu.VMEM((steps,) + state.shape, jnp.bfloat16),
            pltpu.VMEM((steps,) + state.shape, jnp.bfloat16),
            pltpu.SemaphoreType.DMA((count,)),
            pltpu.SemaphoreType.DMA((count,)),
            pltpu.SemaphoreType.DMA((steps,)),
            pltpu.SemaphoreType.DMA((steps,)),
            pltpu.SemaphoreType.DMA,
        ],
        compiler_params=pltpu.CompilerParams(
            collective_id=collective_id, has_side_effects=True, vmem_limit_bytes=24 << 20
        ),
        name=f"early{collective_id}",
    )(x, state)
    return gathered, earlier


def halving_orders(bits):
    count = len(bits)
    first = list(reversed(range(count)))
    heads = [d for d in first if bits[d][0] == "head"]
    others = [d for d in first if bits[d][0] != "head"]
    if not heads or not others:
        return [first, first]
    return [first, heads[:1] + others[:1] + heads[1:] + others[1:]]


def gather_kernel(bits, parts, x_ref, out_ref, send_sem, recv_sem, own_sem):
    count = len(bits)
    width = x_ref.shape[1] // parts
    orders = [list(reversed(order)) for order in halving_orders(bits)]
    mine = [own_bit(item) for item in bits]

    def region(done, part):
        index = tuple(slice(None) if d in done else mine[d] for d in range(count))
        return out_ref.at[index + (slice(None), pl.ds(part * width, width))]

    own = pltpu.make_async_copy(x_ref, out_ref.at[tuple(mine)], own_sem)
    own.start()
    greet(bits)
    copies = [[None] * count for _ in range(parts)]
    for stage in range(count):
        for part in range(parts):
            order = orders[part % 2]
            if stage == 1 and part == 0:
                own.wait()
            if stage:
                copies[part][stage - 1].wait_recv()
            place = region(order[:stage], part)
            source = x_ref.at[:, pl.ds(part * width, width)] if stage == 0 else place
            copy = pltpu.make_async_remote_copy(
                src_ref=source,
                dst_ref=place,
                send_sem=send_sem.at[part, stage],
                recv_sem=recv_sem.at[part, stage],
                device_id=partner(bits[order[stage]]),
                device_id_type=pl.DeviceIdType.MESH,
            )
            copy.start()
            copies[part][stage] = copy
    for part in range(parts):
        copies[part][count - 1].wait_recv()
    for part in range(parts):
        for stage in range(count):
            copies[part][stage].wait_send()


def gather(x, bits, parts, collective_id):
    count = len(bits)
    rows, columns = x.shape
    out = pl.pallas_call(
        functools.partial(gather_kernel, bits, parts),
        out_shape=jax.ShapeDtypeStruct((2,) * count + x.shape, x.dtype),
        in_specs=[pl.BlockSpec(memory_space=pl.ANY)],
        out_specs=pl.BlockSpec(memory_space=pl.ANY),
        scratch_shapes=[
            pltpu.SemaphoreType.DMA((parts, count)),
            pltpu.SemaphoreType.DMA((parts, count)),
            pltpu.SemaphoreType.DMA,
        ],
        compiler_params=pltpu.CompilerParams(collective_id=collective_id, has_side_effects=True),
        name=f"gather{collective_id}",
    )(x)
    return out.reshape((1 << count) * rows, columns)


def reduce_kernel(bits, parts, x_ref, out_ref, keep, *rest):
    count = len(bits)
    received, (send_sem, recv_sem, own_sem) = rest[:count], rest[count:]
    width = x_ref.shape[-1] // parts
    orders = halving_orders(bits)
    mine = [own_bit(item) for item in bits]

    def columns(part):
        return (slice(None), pl.ds(part * width, width))

    def kept(done, part, flip=None):
        return tuple(
            (1 - mine[d]) if d == flip else (mine[d] if d in done else slice(None))
            for d in range(count - 1)
        ) + columns(part)

    whole = (slice(None),) * (count - 1)
    own = []
    for part in range(parts):
        copy = pltpu.make_async_copy(
            x_ref.at[whole + (mine[-1],) + columns(part)],
            keep.at[whole + columns(part)],
            own_sem.at[part],
        )
        copy.start()
        own.append(copy)
    greet(bits)
    copies = [[None] * count for _ in range(parts)]
    for stage in range(count + 1):
        for part in range(parts):
            order = orders[part % 2]
            if stage:
                if stage == 1:
                    own[part].wait()
                copies[part][stage - 1].wait_recv()
                place = kept(order[:stage], part)
                piece = (slice(None),) * (count - stage) + columns(part)
                total = keep[place] + received[stage - 1][piece]
                if stage == count:
                    out_ref[:, pl.ds(part * width, width)] = total
                    continue
                keep[place] = total
            if stage == 0:
                source = x_ref.at[whole + (1 - mine[-1],) + columns(part)]
            else:
                source = keep.at[kept(order[:stage], part, order[stage])]
            landing = (slice(None),) * (count - 1 - stage) + columns(part)
            copy = pltpu.make_async_remote_copy(
                src_ref=source,
                dst_ref=received[stage].at[landing],
                send_sem=send_sem.at[part, stage],
                recv_sem=recv_sem.at[part, stage],
                device_id=partner(bits[order[stage]]),
                device_id_type=pl.DeviceIdType.MESH,
            )
            copy.start()
            copies[part][stage] = copy
    for part in range(parts):
        for stage in range(count):
            copies[part][stage].wait_send()


def reduce_scatter(x, bits, parts, collective_id):
    count = len(bits)
    rows, columns = x.shape[0] >> count, x.shape[1]
    block = (rows, columns)
    return pl.pallas_call(
        functools.partial(reduce_kernel, bits, parts),
        out_shape=jax.ShapeDtypeStruct(block, x.dtype),
        in_specs=[pl.BlockSpec(memory_space=pl.ANY)],
        out_specs=pl.BlockSpec(memory_space=pltpu.VMEM),
        scratch_shapes=[pltpu.VMEM((2,) * (count - 1) + block, x.dtype)]
        + [pltpu.VMEM((2,) * (count - 1 - stage) + block, x.dtype) for stage in range(count)]
        + [
            pltpu.SemaphoreType.DMA((parts, count)),
            pltpu.SemaphoreType.DMA((parts, count)),
            pltpu.SemaphoreType.DMA((parts,)),
        ],
        compiler_params=pltpu.CompilerParams(
            collective_id=collective_id,
            has_side_effects=True,
            vmem_limit_bytes=(3 * x.shape[0] * columns + 16 * rows * columns) + (4 << 20),
        ),
        name=f"reduce{collective_id}",
    )(x.reshape((2,) * count + block))


def expert_tables(both, rows, exp_local, group_size, capacity):
    both = jnp.transpose(both.reshape(-1, 2 * TOP, both.shape[-1])[:, :, :rows], (0, 2, 1))
    both = both.reshape(-1, 2 * TOP)
    groups = both.shape[0] // group_size
    expert_ids = lax.axis_index("seq") * exp_local + jnp.arange(exp_local, dtype=jnp.int32)
    match = both[:, None, :TOP] == expert_ids.astype(jnp.float32)[None, :, None]
    member = jnp.any(match, axis=2).reshape(groups, group_size, exp_local)
    weight = jnp.sum(jnp.where(match, both[:, None, TOP:], 0.0), axis=2)
    weight = weight.reshape(groups, group_size, exp_local)
    lower = jnp.tril(jnp.ones((group_size, group_size), jnp.bfloat16), -1)
    before = jnp.einsum(
        "ts,gsj->gjt", lower, member.astype(jnp.bfloat16), preferred_element_type=jnp.float32
    )
    member_t = jnp.transpose(member, (0, 2, 1))
    weight_t = jnp.transpose(weight, (0, 2, 1))
    places = jnp.arange(capacity, dtype=jnp.float32)
    picks = (before[:, :, None, :] == places[:, None]) & member_t[:, :, None, :]
    row_weight = jnp.sum(jnp.where(picks, weight_t[:, :, None, :], 0.0), axis=3)
    return picks.astype(jnp.bfloat16), row_weight


def on_device(
    hidden_in, attn_gain, w_qkv, out_gain, w_out, moe_gain, routes, gate_weights, w_gate_up, w_down
):
    token_count = hidden_in.shape[0]
    head_count = w_qkv.shape[2] // DH
    seq_size = lax.axis_size("seq")
    head_size = lax.axis_size("head")
    exp_local = w_gate_up.shape[0]
    row_count = token_count // head_size
    capacity = max(2, 9 * row_count * TOP // (8 * EXPERTS))
    blocks = 8
    group_size = blocks * row_count
    resid_in = hidden_in.astype(jnp.float32)
    normed = rms_norm(resid_in, attn_gain).astype(jnp.bfloat16)
    query, keys_local, values_local = (
        jnp.dot(normed, w_qkv[:, c], preferred_element_type=jnp.float32)
        .astype(jnp.bfloat16)
        .reshape(token_count, head_count, DH)
        for c in range(3)
    )
    causal = jnp.tril(jnp.ones((token_count, token_count), jnp.float32))
    scores = (
        jnp.einsum("thd,shd->hts", query, keys_local, preferred_element_type=jnp.float32) * causal
    )
    local_part = jnp.einsum(
        "hts,shd->thd",
        scores.astype(jnp.bfloat16),
        values_local,
        preferred_element_type=jnp.float32,
    )
    own_state = jnp.einsum(
        "thd,the->hde", keys_local, values_local, preferred_element_type=jnp.float32
    )
    both = jnp.concatenate([routes.astype(jnp.float32), gate_weights], axis=1)
    both, earlier = early_exchange(
        jnp.pad(both.T, ((0, 0), (0, -row_count % 128))),
        own_state.reshape(head_count * DH, DH),
        axis_bits("seq") + axis_bits("head"),
        axis_bits("seq"),
        0,
    )
    earlier = earlier.reshape(own_state.shape)
    picks, row_weight = expert_tables(
        both, row_count, exp_local, group_size, blocks * capacity
    )
    remote_part = jnp.einsum(
        "thd,hde->the", query.astype(jnp.float32), earlier, precision=lax.Precision.HIGHEST
    )
    attended = local_part + remote_part
    head_square = jnp.mean(attended * attended, axis=-1, keepdims=True)
    mixed = (attended * lax.rsqrt(head_square + EPSILON)).reshape(
        token_count, head_count * DH
    ) * out_gain
    mixed = mixed.astype(jnp.bfloat16)
    attn_rows = reduce_scatter(
        jnp.dot(mixed, w_out, preferred_element_type=jnp.float32).astype(jnp.bfloat16),
        axis_bits("head"),
        2,
        2,
    ).astype(jnp.float32)
    resid = (
        lax.dynamic_slice_in_dim(resid_in, lax.axis_index("head") * row_count, row_count, 0)
        + attn_rows
    )
    normed2 = rms_norm(resid, moe_gain).astype(jnp.bfloat16)
    everyone = gather(normed2, axis_bits("seq") + axis_bits("head"), 8, 3)
    everyone = everyone.reshape(-1, group_size, D)
    rows_in = jnp.einsum(
        "gjct,gtd->jgcd", picks, everyone, preferred_element_type=jnp.float32
    ).astype(jnp.bfloat16)
    gate_val = jnp.einsum(
        "jgcd,jdf->jgcf", rows_in, w_gate_up[:, 0], preferred_element_type=jnp.float32
    )
    up_val = jnp.einsum(
        "jgcd,jdf->jgcf", rows_in, w_gate_up[:, 1], preferred_element_type=jnp.float32
    )
    weights = jnp.transpose(row_weight, (1, 0, 2))[..., None]
    hidden_units = (jax.nn.silu(gate_val) * up_val * weights).astype(jnp.bfloat16)
    rows_out = jnp.einsum(
        "jgcf,jfd->jgcd", hidden_units, w_down, preferred_element_type=jnp.float32
    ).astype(jnp.bfloat16)
    partial = jnp.einsum(
        "gjct,jgcd->gtd", picks, rows_out, preferred_element_type=jnp.float32
    ).astype(jnp.bfloat16)
    moe_sum = reduce_scatter(
        partial.reshape(-1, D), axis_bits("seq") + axis_bits("head"), 8, 4
    )
    return (resid + moe_sum.astype(jnp.float32)).astype(jnp.bfloat16)


def solution(mesh):
    placed = (
        P("seq", None),
        P(),
        P(None, None, "head"),
        P("head"),
        P("head", None),
        P(),
        P(("seq", "head"), None),
        P(("seq", "head"), None),
        P("seq", None, None, "head"),
        P("seq", "head", None),
    )
    return jax.shard_map(
        on_device, mesh=mesh, in_specs=placed, out_specs=P(("seq", "head"), None), check_vma=False
    )
```
